32 devices in a mesh: frame: 4 (over z), lat: 4 (over y, core), lon: 2 (over x).
Axes of the slice: x: 2, y: 2, z: 4, core: 2. Of those that a mesh axis runs over, the one named last changes fastest.
Arguments:
- frames_in: bfloat16 [16, 32, 64, 512], P('frame', 'lat', 'lon'), may hold values from -6 to 6
- grad_out: bfloat16 [16, 32, 64, 512], P('frame', 'lat', 'lon'), may hold values from -6 to 6
- kernel: bfloat16 [49, 512], replicated, may hold values from -0.875 to 0.875
- w_qkv: bfloat16 [512, 1536], replicated, may hold values from -0.25 to 0.25
- w_out: bfloat16 [512, 512], replicated, may hold values from -0.25 to 0.25
Outputs:
- grad_input: bfloat16 [16, 32, 64, 512], P('frame', 'lat', 'lon')
- grad_proj: float32 [512, 2048], P(('frame', 'lat', 'lon'))
- grad_kernel: float32 [49, 512], replicated
The draws below stay inside these ranges and needn't reach their ends.
All inputs are finite; a program needn't handle non-finite values.
Results may differ from the reference program's by a relative error of at most 0.0098.
Values may be sent and summed in bfloat16 or wider, within the bound.
A program may use at most 128 MiB of HBM per device.

```python
import math
import jax
import jax.numpy as jnp
from jax import lax

CHANNELS = 512
HEADS = 4
FRAMES = 16
KSIZE = 7
TAPS = 49
GRID_LAT = 32
GRID_LON = 64


def levels(key, dims, shards, smallest, top_value):
    loudness, own = 1.0, jax.random.fold_in(key, 6)
    for dim, shards_of in shards:
        draws = jnp.exp(jax.random.uniform(jax.random.fold_in(own, dim), (shards_of,), jnp.float32, smallest / len(shards), top_value / len(shards)))
        loudness = loudness * jnp.repeat(draws, dims[dim] // shards_of).reshape([-1 if axis == dim else 1 for axis in range(len(dims))])
    return loudness


def normal_values(own_key, shape, scale, reach, cuts=(), dtype=jnp.bfloat16):
    entries = jax.random.normal(own_key, shape, jnp.float32) * scale
    if len(cuts) > 0:
        entries = levels(own_key, shape, cuts, -0.22, 0.18) * entries
    return jnp.clip(entries, min=-reach, max=reach).astype(dtype)


def setup_inputs(seed: int = 0) -> dict:
    key_of = jax.random.split(jax.random.key(seed), 6)
    return {
        "frames_in": normal_values(key_of[0], (FRAMES, GRID_LAT, GRID_LON, CHANNELS), 1.0, 6.0, ((0, 4), (1, 4), (2, 2))),
        "grad_out": normal_values(key_of[1], (FRAMES, GRID_LAT, GRID_LON, CHANNELS), 1.0, 6.0, ((0, 4), (1, 4), (2, 2))),
        "kernel": normal_values(key_of[2], (TAPS, CHANNELS), TAPS ** -0.5, 0.875),
        "w_qkv": normal_values(key_of[3], (CHANNELS, 3 * CHANNELS), CHANNELS ** -0.5, 0.25),
        "w_out": normal_values(key_of[4], (CHANNELS, CHANNELS), CHANNELS ** -0.5, 0.25),
    }


def conv_taps(padded, kernel, rows, cols, flipped):
    side = math.isqrt(kernel.shape[0])
    total = jnp.zeros((padded.shape[0], rows, cols, padded.shape[3]), jnp.float32)
    for row_tap in range(side):
        for col_tap in range(side):
            weight = kernel[row_tap * side + col_tap].astype(jnp.float32)
            if flipped:
                start_row = side - 1 - row_tap
                start_col = side - 1 - col_tap
            else:
                start_row = row_tap
                start_col = col_tap
            window = padded[:, start_row:start_row + rows, start_col:start_col + cols, :]
            total = total + weight * window.astype(jnp.float32)
    return total

def tap_products(padded, grad_mixed, side):
    rows = grad_mixed.shape[1]
    cols = grad_mixed.shape[2]
    grad_wide = grad_mixed.astype(jnp.float32)
    terms = []
    for row_tap in range(side):
        for col_tap in range(side):
            window = padded[:, row_tap:row_tap + rows, col_tap:col_tap + cols, :].astype(jnp.float32)
            terms.append(lax.optimization_barrier(jnp.sum(window * grad_wide, axis=(0, 1, 2))))
    return jnp.stack(terms, axis=0)

def attend(projected, grad_rows, w_out, heads):
    frames, count, triple = projected.shape
    width = triple // 3
    depth = width // heads
    scale = depth ** (-0.5)
    queries = projected[:, :, :width].reshape(frames, count, heads, depth).astype(jnp.float32)
    key_rows = projected[:, :, width:2 * width].reshape(frames, count, heads, depth).astype(jnp.float32)
    value_rows = projected[:, :, 2 * width:].reshape(frames, count, heads, depth).astype(jnp.float32)
    scores = jnp.einsum('ithd,jthd->ijht', queries, key_rows) * scale
    raised = jnp.exp(scores)
    probs = raised / lax.optimization_barrier(jnp.sum(raised, axis=1, keepdims=True))
    probs_low = probs.astype(jnp.bfloat16)
    attended = jnp.einsum('ijht,jthd->ithd', probs_low.astype(jnp.float32), value_rows).astype(jnp.bfloat16)
    grad_flat = grad_rows.reshape(frames * count, width)
    grad_att = lax.dot_general(grad_flat, w_out, (((1,), (1,)), ((), ())), preferred_element_type=jnp.float32)
    grad_att = grad_att.astype(jnp.bfloat16).reshape(frames, count, heads, depth).astype(jnp.float32)
    grad_probs = jnp.einsum('ithd,jthd->ijht', grad_att, value_rows)
    inner = lax.optimization_barrier(jnp.sum(probs * grad_probs, axis=1, keepdims=True))
    grad_scores = (probs * (grad_probs - inner) * scale).astype(jnp.bfloat16).astype(jnp.float32)
    grad_query = jnp.einsum('ijht,jthd->ithd', grad_scores, key_rows).astype(jnp.bfloat16)
    grad_key = jnp.einsum('ijht,ithd->jthd', grad_scores, queries).astype(jnp.bfloat16)
    grad_value = jnp.einsum('ijht,ithd->jthd', probs_low.astype(jnp.float32), grad_att).astype(jnp.bfloat16)
    stacked = jnp.concatenate([grad_query.reshape(frames, count, width), grad_key.reshape(frames, count, width), grad_value.reshape(frames, count, width)], axis=2)
    return (stacked, attended.reshape(frames, count, width))

def reference(frames_in, grad_out, kernel, w_qkv, w_out):
    half = KSIZE // 2
    pad_spec = ((0, 0), (half, half), (half, half), (0, 0))
    width = CHANNELS

    def forward_frame(frame):
        padded = jnp.pad(frame[None], pad_spec)
        return conv_taps(padded, kernel, GRID_LAT, GRID_LON, False).astype(jnp.bfloat16)[0]
    mixed = lax.map(forward_frame, frames_in)
    mixed_lat = jnp.transpose(mixed, (1, 0, 2, 3))
    grad_lat = jnp.transpose(grad_out, (1, 0, 2, 3))

    def row_step(carry, item):
        mixed_row, grad_row = item
        mixed_flat = mixed_row.reshape(-1, width)
        projected = jnp.dot(mixed_flat, w_qkv, preferred_element_type=jnp.float32).astype(jnp.bfloat16)
        projected = projected.reshape(FRAMES, GRID_LON, 3 * width)
        stacked, attended = attend(projected, grad_row, w_out, HEADS)
        flat_grad = stacked.reshape(-1, 3 * width)
        grad_mix = lax.dot_general(flat_grad, w_qkv, (((1,), (1,)), ((), ())), preferred_element_type=jnp.float32)
        grad_mix = grad_mix.astype(jnp.bfloat16).reshape(FRAMES, GRID_LON, width)
        qkv_term = lax.dot_general(mixed_flat, flat_grad, (((0,), (0,)), ((), ())), preferred_element_type=jnp.float32)
        out_term = lax.dot_general(attended.reshape(-1, width), grad_row.reshape(-1, width), (((0,), (0,)), ((), ())), preferred_element_type=jnp.float32)
        return ((carry[0] + qkv_term, carry[1] + out_term), grad_mix)
    start = (jnp.zeros((width, 3 * width), jnp.float32), jnp.zeros((width, width), jnp.float32))
    sums, grad_mix_lat = lax.scan(row_step, start, (mixed_lat, grad_lat))
    grad_mixed = jnp.transpose(grad_mix_lat, (1, 0, 2, 3))

    def frame_step(carry, item):
        frame, grad_frame, grad_mix = item
        padded = jnp.pad(frame[None], pad_spec)
        grad_pad = jnp.pad(grad_mix[None], pad_spec)
        adjoint = conv_taps(grad_pad, kernel, GRID_LAT, GRID_LON, True)[0]
        grad_in = (grad_frame.astype(jnp.float32) + adjoint).astype(jnp.bfloat16)
        return (carry + tap_products(padded, grad_mix[None], KSIZE), grad_in)
    kernel_total, grad_input = lax.scan(frame_step, jnp.zeros((TAPS, width), jnp.float32), (frames_in, grad_out, grad_mixed))
    scale = (FRAMES * GRID_LAT * GRID_LON) ** (-0.5)
    grad_proj = jnp.concatenate([sums[0], sums[1]], axis=1) * scale
    return (grad_input, grad_proj, kernel_total * scale)
```

```python
import math

import jax
import jax.numpy as jnp
from jax import lax
from jax.sharding import PartitionSpec as P

HEADS = 4


def extended(block, sides, width):
    for axis, dim in sides:
        count = lax.axis_size(axis)
        forward = [(i, i + 1) for i in range(count - 1)]
        backward = [(target, source) for source, target in forward]
        low = lax.ppermute(
            lax.slice_in_dim(block, block.shape[dim] - width, None, axis=dim), axis, forward
        )
        high = lax.ppermute(lax.slice_in_dim(block, 0, width, axis=dim), axis, backward)
        block = jnp.concatenate([low, block, high], axis=dim)
    return block


def conv_taps(padded, kernel, rows, cols, flipped):
    side = math.isqrt(kernel.shape[0])
    total = jnp.zeros((padded.shape[0], rows, cols, padded.shape[3]), jnp.float32)
    for row_tap in range(side):
        for col_tap in range(side):
            weight = kernel[row_tap * side + col_tap].astype(jnp.float32)
            if flipped:
                start_row = side - 1 - row_tap
                start_col = side - 1 - col_tap
            else:
                start_row = row_tap
                start_col = col_tap
            window = padded[:, start_row : start_row + rows, start_col : start_col + cols, :]
            total = total + weight * window.astype(jnp.float32)
    return total


def tap_products(padded, grad_mixed, side):
    rows = grad_mixed.shape[1]
    cols = grad_mixed.shape[2]
    grad_wide = grad_mixed.astype(jnp.float32)
    terms = []
    for row_tap in range(side):
        for col_tap in range(side):
            window = padded[:, row_tap : row_tap + rows, col_tap : col_tap + cols, :].astype(
                jnp.float32
            )
            terms.append(jnp.sum(window * grad_wide, axis=(0, 1, 2)))
    return jnp.stack(terms, axis=0)


def attend(projected, grad_rows, w_out, heads):
    frames, count, triple = projected.shape
    width = triple // 3
    depth = width // heads
    scale = depth ** (-0.5)
    queries = projected[:, :, :width].reshape(frames, count, heads, depth)
    key_rows = projected[:, :, width : 2 * width].reshape(frames, count, heads, depth)
    value_rows = projected[:, :, 2 * width :].reshape(frames, count, heads, depth)
    scores = (
        jnp.einsum("ithd,jthd->ijht", queries, key_rows, preferred_element_type=jnp.float32) * scale
    )
    raised = jnp.exp(scores)
    probs = raised / jnp.sum(raised, axis=1, keepdims=True)
    probs_low = probs.astype(jnp.bfloat16)
    attended = jnp.einsum(
        "ijht,jthd->ithd", probs_low, value_rows, preferred_element_type=jnp.float32
    ).astype(jnp.bfloat16)
    grad_flat = grad_rows.reshape(frames * count, width)
    grad_att = lax.dot_general(
        grad_flat, w_out, (((1,), (1,)), ((), ())), preferred_element_type=jnp.float32
    )
    grad_att = grad_att.astype(jnp.bfloat16).reshape(frames, count, heads, depth)
    grad_probs = jnp.einsum(
        "ithd,jthd->ijht", grad_att, value_rows, preferred_element_type=jnp.float32
    )
    inner = jnp.sum(probs * grad_probs, axis=1, keepdims=True)
    grad_scores = (probs * (grad_probs - inner) * scale).astype(jnp.bfloat16)
    grad_query = jnp.einsum(
        "ijht,jthd->ithd", grad_scores, key_rows, preferred_element_type=jnp.float32
    ).astype(jnp.bfloat16)
    grad_key = jnp.einsum(
        "ijht,ithd->jthd", grad_scores, queries, preferred_element_type=jnp.float32
    ).astype(jnp.bfloat16)
    grad_value = jnp.einsum(
        "ijht,ithd->jthd", probs_low, grad_att, preferred_element_type=jnp.float32
    ).astype(jnp.bfloat16)
    stacked = jnp.concatenate(
        [
            grad_query.reshape(frames, count, width),
            grad_key.reshape(frames, count, width),
            grad_value.reshape(frames, count, width),
        ],
        axis=2,
    )
    return (stacked, attended.reshape(frames, count, width))


def output_term(attended, spread_grad, width):
    return lax.dot_general(
        attended.reshape(-1, width),
        spread_grad.reshape(-1, width),
        (((0,), (0,)), ((), ())),
        preferred_element_type=jnp.float32,
    )


def swapped(value, axis, bit):
    count = lax.axis_size(axis)
    return lax.ppermute(value, axis, [(i, i ^ bit) for i in range(count)])


def paired_total(value, axes):
    for axis in axes:
        bit = 1
        while bit < lax.axis_size(axis):
            value = value + swapped(value, axis, bit)
            bit *= 2
    return value


def paired_scatter(value, axes, order):
    sizes = [lax.axis_size(axis) for axis in axes]
    digits = []
    for axis, size in zip(axes, sizes):
        bit = size // 2
        while bit >= 1:
            digits.append((axis, bit))
            bit //= 2
    rows, cols = value.shape
    value = value.reshape((2,) * len(digits) + (rows // math.prod(sizes), cols))
    for axis in order:
        bit = 1
        while bit < lax.axis_size(axis):
            dim = digits.index((axis, bit))
            mine = (lax.axis_index(axis) // bit) % 2
            digits.pop(dim)
            away = lax.dynamic_index_in_dim(value, 1 - mine, dim, keepdims=False)
            kept = lax.dynamic_index_in_dim(value, mine, dim, keepdims=False)
            came = swapped(away.astype(jnp.bfloat16), axis, bit)
            value = kept.astype(jnp.float32) + came.astype(jnp.float32)
            bit *= 2
    return value


def on_device(frames_in, grad_out, kernel, w_qkv, w_out):
    local_frames, tile_lat, tile_lon, width = frames_in.shape
    side = math.isqrt(kernel.shape[0])
    half = side // 2
    padded = extended(frames_in, (("lat", 1), ("lon", 2)), half)
    mixed = conv_taps(padded, kernel, tile_lat, tile_lon, False).astype(jnp.bfloat16)
    tokens = tile_lat * tile_lon
    mixed_rows = mixed.reshape(local_frames, tokens, width)
    grad_rows = grad_out.reshape(local_frames, tokens, width)
    spread_mixed, spread_grad = (
        lax.all_to_all(mixed_rows, "frame", split_axis=1, concat_axis=0, tiled=True),
        lax.all_to_all(grad_rows, "frame", split_axis=1, concat_axis=0, tiled=True),
    )
    mixed_flat = spread_mixed.reshape(-1, width)
    projected = jnp.dot(mixed_flat, w_qkv, preferred_element_type=jnp.float32).astype(jnp.bfloat16)
    projected = projected.reshape(spread_mixed.shape[0], spread_mixed.shape[1], 3 * width)
    stacked, attended = attend(projected, spread_grad, w_out, HEADS)
    out_part = output_term(attended, spread_grad, width)
    flat_grad = stacked.reshape(-1, 3 * width)
    token_grad = lax.dot_general(
        flat_grad, w_qkv, (((1,), (1,)), ((), ())), preferred_element_type=jnp.float32
    ).astype(jnp.bfloat16)
    token_grad = token_grad.reshape(spread_mixed.shape)
    grad_mixed = lax.all_to_all(token_grad, "frame", split_axis=0, concat_axis=1, tiled=True)
    qkv_part = lax.dot_general(
        mixed_flat, flat_grad, (((0,), (0,)), ((), ())), preferred_element_type=jnp.float32
    )
    grad_mixed = grad_mixed.reshape(local_frames, tile_lat, tile_lon, width)
    grad_pad = extended(grad_mixed, (("lat", 1), ("lon", 2)), half)
    adjoint = conv_taps(grad_pad, kernel, tile_lat, tile_lon, True)
    grad_input = (grad_out.astype(jnp.float32) + adjoint).astype(jnp.bfloat16)
    kernel_part = tap_products(padded, grad_mixed, side)
    total_cells = (
        local_frames
        * lax.axis_size("frame")
        * tile_lat
        * lax.axis_size("lat")
        * tile_lon
        * lax.axis_size("lon")
    )
    scale = total_cells ** (-0.5)
    grad_kernel = paired_total(kernel_part, ("lat", "lon", "frame")) * scale
    joined = jnp.concatenate([qkv_part, out_part], axis=1)
    grad_proj = paired_scatter(joined, ("frame", "lat", "lon"), ("lat", "lon", "frame")) * scale
    return (grad_input, grad_proj, grad_kernel)


def solution(mesh):
    in_specs = (P("frame", "lat", "lon", None), P("frame", "lat", "lon", None), P(), P(), P())
    out_specs = (P("frame", "lat", "lon", None), P(("frame", "lat", "lon"), None), P())
    return jax.shard_map(
        on_device, mesh=mesh, in_specs=in_specs, out_specs=out_specs, check_vma=False
    )
```

```python
import functools
import math

import jax
import jax.numpy as jnp
from jax import lax
from jax.experimental import pallas as pl
from jax.experimental.pallas import tpu as pltpu
from jax.sharding import PartitionSpec as P

HEADS = 4
PAD = 8
LANES = 128
LIMIT = 40 * 1024 * 1024


def edges(block, width):
    count = lax.axis_size("lat")
    up = [(i, i + 1) for i in range(count - 1)]
    down = [(j, i) for i, j in up]
    rows = block.shape[1]
    low = lax.ppermute(block[:, rows - width :], "lat", up)
    high = lax.ppermute(block[:, :width], "lat", down)
    count = lax.axis_size("lon")
    up = [(i, i + 1) for i in range(count - 1)]
    down = [(j, i) for i, j in up]
    cols = block.shape[2]

    def strip(start):
        parts = [part[:, :, start : start + width] for part in (low, block, high)]
        return jnp.concatenate(parts, axis=1)

    left = lax.ppermute(strip(cols - width), "lon", up)
    right = lax.ppermute(strip(0), "lon", down)
    return low, high, left, right


def fill(scratch, centre, low, high, left, right, half):
    rows, cols = len(centre), centre[0].shape[0]
    for row in range(half):
        scratch[row, PAD : PAD + cols, :] = low[0, row].astype(jnp.float32)
        scratch[row + rows + half, PAD : PAD + cols, :] = high[0, row].astype(jnp.float32)
    for row in range(rows):
        scratch[row + half, PAD : PAD + cols, :] = centre[row].astype(jnp.float32)
    for row in range(rows + 2 * half):
        scratch[row, PAD - half : PAD, :] = left[0, row].astype(jnp.float32)
        scratch[row, PAD + cols : PAD + cols + half, :] = right[0, row].astype(jnp.float32)


def tile_rows(ref):
    if len(ref.shape) == 4:
        return [ref[0, row] for row in range(ref.shape[1])]
    return [ref[part, 0, row] for part in range(ref.shape[0]) for row in range(ref.shape[2])]


def conv_kernel(side, half, has_base, centre, low, high, left, right, weights, *rest):
    out, scratch = rest[-2], rest[-1]
    rows = tile_rows(centre)
    cols = rows[0].shape[0]
    fill(scratch, rows, low, high, left, right, half)
    count = len(rows)
    if has_base:
        totals = [rest[0][0, row].astype(jnp.float32) for row in range(count)]
    else:
        totals = [None] * count
    for col_tap in range(side):
        taps = [
            jnp.broadcast_to(weights[row_tap * side + col_tap], (8, scratch.shape[2]))
            for row_tap in range(side)
        ]
        first = PAD - half + col_tap
        for source in range(count + 2 * half):
            window = scratch[source, first : first + cols, :].reshape(cols // 8, 8, -1)
            for row_tap in range(side):
                row = source - row_tap
                if 0 <= row < count:
                    term = (window * taps[row_tap][None]).reshape(cols, -1)
                    totals[row] = term if totals[row] is None else totals[row] + term
    for row in range(count):
        value = totals[row].astype(out.dtype)
        if len(out.shape) == 4:
            out[0, row] = value
        else:
            out[row // out.shape[2], 0, row % out.shape[2]] = value


def tap_kernel(side, half, centre, low, high, left, right, grads, out, scratch, sums):
    frame = pl.program_id(1)
    rows = tile_rows(centre)
    cols = rows[0].shape[0]
    fill(scratch, rows, low, high, left, right, half)
    count = len(rows)

    @pl.when(frame == 0)
    def _():
        sums[...] = jnp.zeros_like(sums)

    wide = [row.astype(jnp.float32) for row in tile_rows(grads)]
    for col_tap in range(side):
        first = PAD - half + col_tap
        parts = [None] * side
        for source in range(count + 2 * half):
            window = scratch[source, first : first + cols, :]
            for row_tap in range(side):
                row = source - row_tap
                if 0 <= row < count:
                    term = jnp.sum((window * wide[row]).reshape(cols // 8, 8, -1), axis=0)
                    parts[row_tap] = term if parts[row_tap] is None else parts[row_tap] + term
        for row_tap in range(side):
            sums[row_tap * side + col_tap] += parts[row_tap]

    @pl.when(frame == pl.num_programs(1) - 1)
    def _():
        out[...] = jnp.sum(sums[...], axis=1)


def frame_spec(array, lanes, flip):
    if array.ndim == 4:
        shape = (1,) + array.shape[1:3] + (lanes,)
        place = lambda f, c: (f, 0, 0, c)
    else:
        shape = (array.shape[0], 1) + array.shape[2:4] + (lanes,)
        place = lambda f, c: (0, f, 0, 0, c)
    if flip:
        return pl.BlockSpec(shape, lambda c, f: place(f, c))
    return pl.BlockSpec(shape, place)


def padded_scratch(block, half, lanes):
    rows = block.shape[1] if block.ndim == 4 else block.shape[0] * block.shape[2]
    cols = block.shape[-2]
    return pltpu.VMEM((rows + 2 * half, cols + 2 * PAD, lanes), jnp.float32)


def conv_call(block, halo, weights, base, spread):
    frames = halo[0].shape[0]
    width = block.shape[-1]
    lanes = min(LANES, width)
    side = math.isqrt(weights.shape[0])
    half = side // 2
    rows = block.shape[1] if block.ndim == 4 else block.shape[0] * block.shape[2]
    cols = block.shape[-2]
    if spread is None:
        out = jax.ShapeDtypeStruct((frames, rows, cols, width), block.dtype)
    else:
        out = jax.ShapeDtypeStruct((spread, frames, rows // spread, cols, width), block.dtype)
    operands = [block, *halo]
    specs = [frame_spec(value, lanes, False) for value in operands]
    operands.append(weights.astype(jnp.float32)[:, None, :])
    specs.append(pl.BlockSpec((weights.shape[0], 1, lanes), lambda f, c: (0, 0, c)))
    if base is not None:
        operands.append(base)
        specs.append(frame_spec(base, lanes, False))
    flops = 2 * frames * rows * cols * width * weights.shape[0]
    return pl.pallas_call(
        functools.partial(conv_kernel, side, half, base is not None),
        grid=(frames, width // lanes),
        in_specs=specs,
        out_specs=frame_spec(out, lanes, False),
        out_shape=out,
        scratch_shapes=[padded_scratch(block, half, lanes)],
        compiler_params=pltpu.CompilerParams(vmem_limit_bytes=LIMIT),
        cost_estimate=pl.CostEstimate(flops=flops, bytes_accessed=4 * block.size, transcendentals=0),
    )(*operands)


def tap_call(block, halo, grads, side):
    frames, rows, cols, width = block.shape
    lanes = min(LANES, width)
    half = side // 2
    operands = [block, *halo, grads]
    flops = 2 * frames * rows * cols * width * side * side
    return pl.pallas_call(
        functools.partial(tap_kernel, side, half),
        grid=(width // lanes, frames),
        in_specs=[frame_spec(value, lanes, True) for value in operands],
        out_specs=pl.BlockSpec((side * side, lanes), lambda c, f: (0, c)),
        out_shape=jax.ShapeDtypeStruct((side * side, width), jnp.float32),
        scratch_shapes=[
            padded_scratch(block, half, lanes),
            pltpu.VMEM((side * side, 8, lanes), jnp.float32),
        ],
        compiler_params=pltpu.CompilerParams(vmem_limit_bytes=LIMIT),
        cost_estimate=pl.CostEstimate(flops=flops, bytes_accessed=4 * block.size, transcendentals=0),
    )(*operands)


def product(left, right, left_dim, right_dim):
    return lax.dot_general(
        left, right, (((left_dim,), (right_dim,)), ((), ())), preferred_element_type=jnp.float32
    )


def attend_kernel(
    heads, mixed, grads, w_qkv, w_out, token_grad, qkv_part, out_part, stacked, attended
):
    frames, cells, width = mixed.shape
    rows = frames * cells
    depth = width // heads
    scale = depth ** (-0.5)
    low = jnp.bfloat16

    @pl.when(pl.program_id(0) == 0)
    def _():
        qkv_part[...] = jnp.zeros_like(qkv_part)
        out_part[...] = jnp.zeros_like(out_part)

    tokens = mixed[...].reshape(rows, width)
    cotangents = grads[...].reshape(rows, width)
    projected = product(tokens, w_qkv[...], 1, 0).astype(low)
    grad_att = product(cotangents, w_out[...], 1, 1).astype(low)
    mine = lax.rem(lax.broadcasted_iota(jnp.int32, (rows, rows), 0), cells)
    theirs = lax.rem(lax.broadcasted_iota(jnp.int32, (rows, rows), 1), cells)
    same = mine == theirs
    for head in range(heads):
        start = head * depth
        queries = projected[:, start : start + depth]
        keys = projected[:, width + start : width + start + depth]
        values = projected[:, 2 * width + start : 2 * width + start + depth]
        grad_head = grad_att[:, start : start + depth]
        scores = product(queries, keys, 1, 1) * scale
        raised = jnp.where(same, jnp.exp(scores), 0.0)
        probs = raised / jnp.sum(raised, axis=1, keepdims=True)
        probs_low = probs.astype(low)
        attended[:, start : start + depth] = product(probs_low, values, 1, 0).astype(low)
        grad_probs = product(grad_head, values, 1, 1)
        inner = jnp.sum(probs * grad_probs, axis=1, keepdims=True)
        grad_scores = (probs * (grad_probs - inner) * scale).astype(low)
        stacked[:, start : start + depth] = product(grad_scores, keys, 1, 0).astype(low)
        stacked[:, width + start : width + start + depth] = product(
            grad_scores, queries, 0, 0
        ).astype(low)
        stacked[:, 2 * width + start : 2 * width + start + depth] = product(
            probs_low, grad_head, 0, 0
        ).astype(low)
    token_grad[...] = product(stacked[...], w_qkv[...], 1, 1).astype(low).reshape(token_grad.shape)
    qkv_part[...] += product(tokens, stacked[...], 0, 0)
    out_part[...] += product(attended[...], cotangents, 0, 0)


def attend_call(mixed, grads, w_qkv, w_out, heads):
    frames, count, width = mixed.shape
    cells = min(16, count)
    rows = frames * cells
    wide = w_qkv.shape[1]
    block = pl.BlockSpec((frames, cells, width), lambda g: (0, g, 0))

    def whole(*shape):
        return pl.BlockSpec(shape, lambda g: (0, 0))

    return pl.pallas_call(
        functools.partial(attend_kernel, heads),
        grid=(count // cells,),
        in_specs=[block, block, whole(width, wide), whole(width, width)],
        out_specs=[block, whole(width, wide), whole(width, width)],
        out_shape=[
            jax.ShapeDtypeStruct(mixed.shape, jnp.bfloat16),
            jax.ShapeDtypeStruct((width, wide), jnp.float32),
            jax.ShapeDtypeStruct((width, width), jnp.float32),
        ],
        scratch_shapes=[
            pltpu.VMEM((rows, wide), jnp.bfloat16),
            pltpu.VMEM((rows, width), jnp.bfloat16),
        ],
        compiler_params=pltpu.CompilerParams(vmem_limit_bytes=LIMIT),
    )(mixed, grads, w_qkv, w_out)


def swapped(value, axis, bit):
    count = lax.axis_size(axis)
    return lax.ppermute(value, axis, [(i, i ^ bit) for i in range(count)])


def paired_total(value, axes):
    for axis in axes:
        bit = 1
        while bit < lax.axis_size(axis):
            value = value + swapped(value, axis, bit)
            bit *= 2
    return value


def paired_scatter(value, axes, order):
    sizes = [lax.axis_size(axis) for axis in axes]
    digits = []
    for axis, size in zip(axes, sizes):
        bit = size // 2
        while bit >= 1:
            digits.append((axis, bit))
            bit //= 2
    rows, cols = value.shape
    value = value.reshape((2,) * len(digits) + (rows // math.prod(sizes), cols))
    for axis in order:
        bit = 1
        while bit < lax.axis_size(axis):
            dim = digits.index((axis, bit))
            mine = (lax.axis_index(axis) // bit) % 2
            digits.pop(dim)
            away = lax.dynamic_index_in_dim(value, 1 - mine, dim, keepdims=False)
            kept = lax.dynamic_index_in_dim(value, mine, dim, keepdims=False)
            came = swapped(away.astype(jnp.bfloat16), axis, bit)
            value = kept.astype(jnp.float32) + came.astype(jnp.float32)
            bit *= 2
    return value


def on_device(frames_in, grad_out, kernel, w_qkv, w_out):
    local_frames, tile_lat, tile_lon, width = frames_in.shape
    side = math.isqrt(kernel.shape[0])
    half = side // 2
    parts = lax.axis_size("frame")
    halo = edges(frames_in, half)
    share = tile_lat // parts
    grad_parts = grad_out.reshape(local_frames, parts, share, tile_lon, width)
    spread_grad = lax.all_to_all(grad_parts.transpose(1, 0, 2, 3, 4), "frame", 0, 0)
    mixed = conv_call(frames_in, halo, kernel, None, parts)
    spread_mixed = lax.all_to_all(mixed, "frame", 0, 0)
    clip = (parts * local_frames, share * tile_lon, width)
    token_grad, qkv_part, out_part = attend_call(
        spread_mixed.reshape(clip), spread_grad.reshape(clip), w_qkv, w_out, HEADS
    )
    grad_mixed = lax.all_to_all(token_grad.reshape(mixed.shape), "frame", 0, 0)
    kernel_part = tap_call(frames_in, halo, grad_mixed, side)
    grad_rows = grad_mixed.transpose(1, 0, 2, 3, 4).reshape(frames_in.shape)
    grad_halo = edges(grad_rows, half)
    grad_input = conv_call(grad_mixed, grad_halo, kernel[::-1], grad_out, None)
    total_cells = (
        local_frames
        * lax.axis_size("frame")
        * tile_lat
        * lax.axis_size("lat")
        * tile_lon
        * lax.axis_size("lon")
    )
    scale = total_cells ** (-0.5)
    grad_kernel = paired_total(kernel_part, ("lat", "lon", "frame")) * scale
    joined = jnp.concatenate([qkv_part, out_part], axis=1)
    grad_proj = paired_scatter(joined, ("frame", "lat", "lon"), ("lat", "lon", "frame")) * scale
    return (grad_input, grad_proj, grad_kernel)


def solution(mesh):
    in_specs = (P("frame", "lat", "lon", None), P("frame", "lat", "lon", None), P(), P(), P())
    out_specs = (P("frame", "lat", "lon", None), P(("frame", "lat", "lon"), None), P())
    return jax.shard_map(
        on_device, mesh=mesh, in_specs=in_specs, out_specs=out_specs, check_vma=False
    )
```

```python
import functools
import math

import jax
import jax.numpy as jnp
from jax import lax
from jax.experimental import pallas as pl
from jax.experimental.pallas import tpu as pltpu
from jax.sharding import PartitionSpec as P

HEADS = 4
PAD = 8
LANES = 128
LIMIT = 40 * 1024 * 1024


def row_edges(block, width):
    count = lax.axis_size("lat")
    up = [(i, i + 1) for i in range(count - 1)]
    down = [(j, i) for i, j in up]
    rows = block.shape[1]
    low = lax.ppermute(block[:, rows - width :], "lat", up)
    high = lax.ppermute(block[:, :width], "lat", down)
    return low, high


def col_edges(block, low, high, width):
    count = lax.axis_size("lon")
    up = [(i, i + 1) for i in range(count - 1)]
    down = [(j, i) for i, j in up]
    cols = block.shape[2]

    def strip(start):
        parts = [part[:, :, start : start + width] for part in (low, block, high)]
        return jnp.concatenate(parts, axis=1)

    left = lax.ppermute(strip(cols - width), "lon", up)
    right = lax.ppermute(strip(0), "lon", down)
    return left, right


def fill(scratch, centre, low, high, left, right, half):
    rows, cols = len(centre), centre[0].shape[0]
    for row in range(half):
        scratch[row, PAD : PAD + cols, :] = low[0, row].astype(jnp.float32)
        scratch[row + rows + half, PAD : PAD + cols, :] = high[0, row].astype(jnp.float32)
    for row in range(rows):
        scratch[row + half, PAD : PAD + cols, :] = centre[row].astype(jnp.float32)
    for row in range(rows + 2 * half):
        scratch[row, PAD - half : PAD, :] = left[0, row].astype(jnp.float32)
        scratch[row, PAD + cols : PAD + cols + half, :] = right[0, row].astype(jnp.float32)


def tile_rows(ref):
    if len(ref.shape) == 4:
        return [ref[0, row] for row in range(ref.shape[1])]
    return [ref[part, 0, row] for part in range(ref.shape[0]) for row in range(ref.shape[2])]


def conv_kernel(side, half, has_base, centre, low, high, left, right, weights, *rest):
    out, scratch = rest[-2], rest[-1]
    rows = tile_rows(centre)
    cols = rows[0].shape[0]
    fill(scratch, rows, low, high, left, right, half)
    count = len(rows)
    if has_base:
        totals = [rest[0][0, row].astype(jnp.float32) for row in range(count)]
    else:
        totals = [None] * count
    for col_tap in range(side):
        taps = [
            jnp.broadcast_to(weights[row_tap * side + col_tap], (8, scratch.shape[2]))
            for row_tap in range(side)
        ]
        first = PAD - half + col_tap
        for source in range(count + 2 * half):
            window = scratch[source, first : first + cols, :].reshape(cols // 8, 8, -1)
            for row_tap in range(side):
                row = source - row_tap
                if 0 <= row < count:
                    term = (window * taps[row_tap][None]).reshape(cols, -1)
                    totals[row] = term if totals[row] is None else totals[row] + term
    for row in range(count):
        value = totals[row].astype(out.dtype)
        if len(out.shape) == 4:
            out[0, row] = value
        else:
            out[row // out.shape[2], 0, row % out.shape[2]] = value


def tap_kernel(side, half, centre, low, high, left, right, grads, out, scratch, sums):
    frame = pl.program_id(1)
    rows = tile_rows(centre)
    cols = rows[0].shape[0]
    fill(scratch, rows, low, high, left, right, half)
    count = len(rows)

    @pl.when(frame == 0)
    def _():
        sums[...] = jnp.zeros_like(sums)

    wide = [row.astype(jnp.float32) for row in tile_rows(grads)]
    for col_tap in range(side):
        first = PAD - half + col_tap
        parts = [None] * side
        for source in range(count + 2 * half):
            window = scratch[source, first : first + cols, :]
            for row_tap in range(side):
                row = source - row_tap
                if 0 <= row < count:
                    term = jnp.sum((window * wide[row]).reshape(cols // 8, 8, -1), axis=0)
                    parts[row_tap] = term if parts[row_tap] is None else parts[row_tap] + term
        for row_tap in range(side):
            sums[row_tap * side + col_tap] += parts[row_tap]

    @pl.when(frame == pl.num_programs(1) - 1)
    def _():
        out[...] = jnp.sum(sums[...], axis=1)


def frame_spec(array, lanes, flip, offset=0):
    if array.ndim == 4:
        shape = (1,) + array.shape[1:3] + (lanes,)
        place = lambda f, c: (f, 0, 0, c)
    else:
        shape = (array.shape[0], 1) + array.shape[2:4] + (lanes,)
        place = lambda f, c: (0, f, 0, 0, c)
    if flip:
        return pl.BlockSpec(shape, lambda c, f: place(f, c + offset))
    return pl.BlockSpec(shape, place)


def padded_scratch(block, half, lanes):
    rows = block.shape[1] if block.ndim == 4 else block.shape[0] * block.shape[2]
    cols = block.shape[-2]
    return pltpu.VMEM((rows + 2 * half, cols + 2 * PAD, lanes), jnp.float32)


def conv_call(block, halo, weights, base, spread):
    frames = halo[0].shape[0]
    width = block.shape[-1]
    lanes = min(LANES, width)
    side = math.isqrt(weights.shape[0])
    half = side // 2
    rows = block.shape[1] if block.ndim == 4 else block.shape[0] * block.shape[2]
    cols = block.shape[-2]
    if spread is None:
        out = jax.ShapeDtypeStruct((frames, rows, cols, width), block.dtype)
    else:
        out = jax.ShapeDtypeStruct((spread, frames, rows // spread, cols, width), block.dtype)
    operands = [block, *halo]
    specs = [frame_spec(value, lanes, False) for value in operands]
    operands.append(weights.astype(jnp.float32)[:, None, :])
    specs.append(pl.BlockSpec((weights.shape[0], 1, lanes), lambda f, c: (0, 0, c)))
    if base is not None:
        operands.append(base)
        specs.append(frame_spec(base, lanes, False))
    flops = 2 * frames * rows * cols * width * weights.shape[0]
    return pl.pallas_call(
        functools.partial(conv_kernel, side, half, base is not None),
        grid=(frames, width // lanes),
        in_specs=specs,
        out_specs=frame_spec(out, lanes, False),
        out_shape=out,
        scratch_shapes=[padded_scratch(block, half, lanes)],
        compiler_params=pltpu.CompilerParams(vmem_limit_bytes=LIMIT),
        cost_estimate=pl.CostEstimate(flops=flops, bytes_accessed=4 * block.size, transcendentals=0),
    )(*operands)


def tap_call(block, halo, grads, side, part, parts):
    frames, rows, cols, width = block.shape
    lanes = min(LANES, width)
    blocks = width // lanes // parts
    half = side // 2
    operands = [block, *halo, grads]
    flops = 2 * frames * rows * cols * width * side * side // parts
    return pl.pallas_call(
        functools.partial(tap_kernel, side, half),
        grid=(blocks, frames),
        in_specs=[frame_spec(value, lanes, True, part * blocks) for value in operands],
        out_specs=pl.BlockSpec((side * side, lanes), lambda c, f: (0, c)),
        out_shape=jax.ShapeDtypeStruct((side * side, blocks * lanes), jnp.float32),
        scratch_shapes=[
            padded_scratch(block, half, lanes),
            pltpu.VMEM((side * side, 8, lanes), jnp.float32),
        ],
        compiler_params=pltpu.CompilerParams(vmem_limit_bytes=LIMIT),
        cost_estimate=pl.CostEstimate(flops=flops, bytes_accessed=4 * block.size, transcendentals=0),
    )(*operands)


def product(left, right, left_dim, right_dim):
    return lax.dot_general(
        left, right, (((left_dim,), (right_dim,)), ((), ())), preferred_element_type=jnp.float32
    )


def attend_kernel(
    heads, mixed, grads, w_qkv, w_out, token_grad, qkv_part, out_part, stacked, attended
):
    frames, cells, width = mixed.shape
    rows = frames * cells
    depth = width // heads
    scale = depth ** (-0.5)
    low = jnp.bfloat16

    @pl.when(pl.program_id(0) == 0)
    def _():
        qkv_part[...] = jnp.zeros_like(qkv_part)
        out_part[...] = jnp.zeros_like(out_part)

    tokens = mixed[...].reshape(rows, width)
    cotangents = grads[...].reshape(rows, width)
    projected = product(tokens, w_qkv[...], 1, 0).astype(low)
    grad_att = product(cotangents, w_out[...], 1, 1).astype(low)
    mine = lax.rem(lax.broadcasted_iota(jnp.int32, (rows, rows), 0), cells)
    theirs = lax.rem(lax.broadcasted_iota(jnp.int32, (rows, rows), 1), cells)
    same = mine == theirs
    for head in range(heads):
        start = head * depth
        queries = projected[:, start : start + depth]
        keys = projected[:, width + start : width + start + depth]
        values = projected[:, 2 * width + start : 2 * width + start + depth]
        grad_head = grad_att[:, start : start + depth]
        scores = product(queries, keys, 1, 1) * scale
        raised = jnp.where(same, jnp.exp(scores), 0.0)
        probs = raised / jnp.sum(raised, axis=1, keepdims=True)
        probs_low = probs.astype(low)
        attended[:, start : start + depth] = product(probs_low, values, 1, 0).astype(low)
        grad_probs = product(grad_head, values, 1, 1)
        inner = jnp.sum(probs * grad_probs, axis=1, keepdims=True)
        grad_scores = (probs * (grad_probs - inner) * scale).astype(low)
        stacked[:, start : start + depth] = product(grad_scores, keys, 1, 0).astype(low)
        stacked[:, width + start : width + start + depth] = product(
            grad_scores, queries, 0, 0
        ).astype(low)
        stacked[:, 2 * width + start : 2 * width + start + depth] = product(
            probs_low, grad_head, 0, 0
        ).astype(low)
    token_grad[...] = product(stacked[...], w_qkv[...], 1, 1).astype(low).reshape(token_grad.shape)
    qkv_part[...] += product(tokens, stacked[...], 0, 0)
    out_part[...] += product(attended[...], cotangents, 0, 0)


def attend_call(mixed, grads, w_qkv, w_out, heads):
    frames, count, width = mixed.shape
    cells = min(16, count)
    rows = frames * cells
    wide = w_qkv.shape[1]
    block = pl.BlockSpec((frames, cells, width), lambda g: (0, g, 0))

    def whole(*shape):
        return pl.BlockSpec(shape, lambda g: (0, 0))

    return pl.pallas_call(
        functools.partial(attend_kernel, heads),
        grid=(count // cells,),
        in_specs=[block, block, whole(width, wide), whole(width, width)],
        out_specs=[block, whole(width, wide), whole(width, width)],
        out_shape=[
            jax.ShapeDtypeStruct(mixed.shape, jnp.bfloat16),
            jax.ShapeDtypeStruct((width, wide), jnp.float32),
            jax.ShapeDtypeStruct((width, width), jnp.float32),
        ],
        scratch_shapes=[
            pltpu.VMEM((rows, wide), jnp.bfloat16),
            pltpu.VMEM((rows, width), jnp.bfloat16),
        ],
        compiler_params=pltpu.CompilerParams(vmem_limit_bytes=LIMIT),
    )(mixed, grads, w_qkv, w_out)


def swapped(value, axis, bit):
    count = lax.axis_size(axis)
    return lax.ppermute(value, axis, [(i, i ^ bit) for i in range(count)])


def paired_total(value, axes):
    for axis in axes:
        bit = 1
        while bit < lax.axis_size(axis):
            value = value + swapped(value, axis, bit)
            bit *= 2
    return value


def scatter_digits(axes):
    digits = []
    for axis in axes:
        bit = lax.axis_size(axis) // 2
        while bit >= 1:
            digits.append((axis, bit))
            bit //= 2
    return digits


def paired_scatter(value, digits, order):
    digits = list(digits)
    for axis in order:
        bit = 1
        while bit < lax.axis_size(axis):
            dim = digits.index((axis, bit))
            mine = (lax.axis_index(axis) // bit) % 2
            digits.pop(dim)
            away = lax.dynamic_index_in_dim(value, 1 - mine, dim, keepdims=False)
            kept = lax.dynamic_index_in_dim(value, mine, dim, keepdims=False)
            came = swapped(away.astype(jnp.bfloat16), axis, bit)
            value = kept.astype(jnp.float32) + came.astype(jnp.float32)
            bit *= 2
    return value, digits


def on_device(frames_in, grad_out, kernel, w_qkv, w_out):
    local_frames, tile_lat, tile_lon, width = frames_in.shape
    side = math.isqrt(kernel.shape[0])
    half = side // 2
    parts = lax.axis_size("frame")
    halo = row_edges(frames_in, half)
    halo = halo + col_edges(frames_in, *halo, half)
    share = tile_lat // parts
    grad_parts = grad_out.reshape(local_frames, parts, share, tile_lon, width)
    spread_grad = lax.all_to_all(grad_parts.transpose(1, 0, 2, 3, 4), "frame", 0, 0)
    mixed = conv_call(frames_in, halo, kernel, None, parts)
    spread_mixed = lax.all_to_all(mixed, "frame", 0, 0)
    clip = (parts * local_frames, share * tile_lon, width)
    token_grad, qkv_part, out_part = attend_call(
        spread_mixed.reshape(clip), spread_grad.reshape(clip), w_qkv, w_out, HEADS
    )
    grad_mixed = lax.all_to_all(token_grad.reshape(mixed.shape), "frame", 0, 0)
    joined = jnp.concatenate([qkv_part, out_part], axis=1)
    digits = scatter_digits(("frame", "lat", "lon"))
    blocks = joined.reshape((2,) * len(digits) + (-1, joined.shape[1]))
    sums, digits = paired_scatter(blocks, digits, ("lat", "lon"))
    grad_mixed, sums = lax.optimization_barrier((grad_mixed, sums))
    grad_rows = grad_mixed.transpose(1, 0, 2, 3, 4).reshape(frames_in.shape)
    low, high = row_edges(grad_rows, half)
    first = tap_call(frames_in, halo, grad_mixed, side, 0, 2)
    low, high, first, sums = lax.optimization_barrier((low, high, first, sums))
    left, right = col_edges(grad_rows, low, high, half)
    later_grads, _ = lax.optimization_barrier((grad_mixed, low))
    second = tap_call(frames_in, halo, later_grads, side, 1, 2)
    kernel_part = jnp.concatenate([first, second], axis=1)
    kernel_part, left, right = lax.optimization_barrier((kernel_part, left, right))
    grad_input = conv_call(
        grad_mixed, (low, high, left, right), kernel[::-1], grad_out, None
    )
    total_cells = (
        local_frames
        * lax.axis_size("frame")
        * tile_lat
        * lax.axis_size("lat")
        * tile_lon
        * lax.axis_size("lon")
    )
    scale = total_cells ** (-0.5)
    grad_kernel = paired_total(kernel_part, ("lat", "lon", "frame")) * scale
    sums, digits = paired_scatter(sums, digits, ("frame",))
    grad_proj = sums * scale
    return (grad_input, grad_proj, grad_kernel)


def solution(mesh):
    in_specs = (P("frame", "lat", "lon", None), P("frame", "lat", "lon", None), P(), P(), P())
    out_specs = (P("frame", "lat", "lon", None), P(("frame", "lat", "lon"), None), P())
    return jax.shard_map(
        on_device, mesh=mesh, in_specs=in_specs, out_specs=out_specs, check_vma=False
    )
```
